32 devices in a mesh: row: 4 (over y, x), col: 8 (over z, core).
Axes of the slice: x: 2, y: 2, z: 4, core: 2. Of those that a mesh axis runs over, the one named last changes fastest.
Arguments:
- tokens: bfloat16 [768, 16384], P('col', 'row'), may hold values from -80 to 80
- draft_counts: int32 [192], replicated, may hold values from 1 to 4
- exit_layers: int32 [192], replicated, may hold values from 0 to 3
- exit_gains: float32 [4, 16384], P(None, 'row'), may hold values from 0.25 to 1.75
- gate_weight: bfloat16 [16384, 26624], P('row', 'col'), may hold values from -0.046875 to 0.046875
- up_weight: bfloat16 [16384, 26624], P('row', 'col'), may hold values from -0.046875 to 0.046875
- down_weight: bfloat16 [26624, 16384], P('col', 'row'), may hold values from -0.0390625 to 0.0390625
Outputs:
- mixed: bfloat16 [768, 16384], P('col', 'row')
The draws below stay inside these ranges and needn't reach their ends.
All inputs are finite; a program needn't handle non-finite values.
Results may differ from the reference program's by a relative error of at most 0.0065.
Values may be sent and summed in bfloat16 or wider, within the bound.
No kernel may reach another device: no remote copies, remote signals or barrier semaphores. Data moves between devices by JAX's collectives and lax.ppermute only.
A program may use at most 192 MiB of HBM per device.

```python
import jax
import jax.numpy as jnp
from jax import lax

D = 16384
FFW = 26624
SEQS = 192
DRAFT = 4
EXITS = 4
ROWS = 768


def draw_tokens(key, part):
    key = jax.random.fold_in(key, 7)
    first, second = jax.random.split(key)
    place = jnp.arange(D, dtype=jnp.float32) / (D - 1)
    column_scale = 0.4 * jnp.exp(jnp.log(10.0) * place)
    base = jnp.clip(jax.random.normal(first, (ROWS, D), jnp.float32), -6.0, 6.0)
    row_scale = jnp.exp(jax.random.uniform(second, (ROWS, 1), jnp.float32, jnp.log(0.3), jnp.log(3.0)))
    return (base * row_scale * column_scale[None, :]).astype(jnp.bfloat16)


def place_ends(drawn, own_key, smallest, top_value):
    longest = drawn.shape.index(max(drawn.shape))
    spots = []
    for shift in (0, 1):
        where = [jax.random.randint(jax.random.fold_in(own_key, axis), (), 0, length) for axis, length in enumerate(drawn.shape)]
        where[longest] = (where[longest] + shift) % drawn.shape[longest]
        spots.append(tuple(where))
    return drawn.at[spots[0]].set(smallest).at[spots[1]].set(top_value)


def levels(rng, dims, shards, least, high):
    def one(axis_at, shards_of):
        draws = jax.random.uniform(jax.random.fold_in(jax.random.fold_in(rng, 6), axis_at), (shards_of,), jnp.float32, least / len(shards), high / len(shards))
        return jnp.repeat(jnp.exp(draws), dims[axis_at] // shards_of).reshape((-1,) + (1,) * (len(dims) - axis_at - 1))

    gain = one(*shards[0])
    for cut in shards[1:]:
        gain = gain * one(*cut)
    return gain


def bell_draw(stream_key, dims, width, bound, pieces=(), held_as=jnp.bfloat16):
    gain = levels(stream_key, dims, pieces, -0.22, 0.18) if pieces else 1.0
    array = jax.random.normal(stream_key, dims, jnp.float32) * width * gain
    return jnp.minimum(jnp.maximum(array, -bound), bound).astype(held_as)


def setup_inputs(seed: int = 0) -> dict:
    splits = jax.random.split(jax.random.key(seed), 8)
    return {
        "tokens": draw_tokens(jax.random.fold_in(splits[7], 71), 0),
        "draft_counts": place_ends(jax.random.randint(splits[1], (SEQS,), 1, DRAFT + 1), jax.random.fold_in(splits[1], 1), 1, DRAFT).astype(jnp.int32),
        "exit_layers": place_ends(jax.random.randint(splits[2], (SEQS,), 0, EXITS), jax.random.fold_in(splits[2], 1), 0, EXITS - 1).astype(jnp.int32),
        "exit_gains": jnp.clip(1.0 + 0.15 * jax.random.normal(splits[3], (EXITS, D), jnp.float32), 0.25, 1.75),
        "gate_weight": bell_draw(splits[4], (D, FFW), D ** -0.5, 0.046875, ((0, 4), (1, 8))),
        "up_weight": bell_draw(splits[5], (D, FFW), D ** -0.5, 0.046875, ((0, 4), (1, 8))),
        "down_weight": bell_draw(splits[6], (FFW, D), FFW ** -0.5, 0.0390625, ((0, 8), (1, 4))),
    }


def reference(tokens, draft_counts, exit_layers, exit_gains, gate_weight, up_weight, down_weight):
    values = tokens.astype(jnp.float32)
    squares = lax.optimization_barrier(jnp.sum(values * values, axis=1))
    scale = lax.rsqrt(squares / D + 1e-05)
    row_exit = jnp.repeat(exit_layers, DRAFT)
    gained = (values * exit_gains[row_exit]).astype(jnp.bfloat16)
    gate = jnp.dot(gained, gate_weight, preferred_element_type=jnp.float32) * scale[:, None]
    up = jnp.dot(gained, up_weight, preferred_element_type=jnp.float32) * scale[:, None]
    hidden = (jax.nn.silu(gate) * up).astype(jnp.bfloat16)
    down = jnp.dot(hidden, down_weight, preferred_element_type=jnp.float32)
    slots = jnp.arange(ROWS, dtype=jnp.int32) % DRAFT
    live = slots < jnp.repeat(draft_counts, DRAFT)
    return jnp.where(live[:, None], down, 0.0).astype(jnp.bfloat16)
```

```python
import functools

import jax
import jax.numpy as jnp
from jax import lax
from jax.sharding import PartitionSpec as P

DRAFT = 4
LANES = 128
F32, BF16 = jnp.float32, jnp.bfloat16


def ring_order(chips):
    return [0] + list(range(1, chips, 2)) + list(range(chips - 2 + chips % 2, 0, -2))


def take(array, axis, part):
    size = array.shape[axis] // 2
    return lax.dynamic_slice_in_dim(array, part * size, size, axis)


def joined(mine, theirs, bit, axis):
    low = jnp.where(bit == 0, mine, theirs)
    high = jnp.where(bit == 0, theirs, mine)
    return jnp.concatenate([low, high], axis)


def partner(array, bit, devices):
    return lax.ppermute(array, "row", [(i, i ^ (1 << bit)) for i in range(devices)])


def reduce_parts(array, order, devices):
    me = lax.axis_index("row")
    for bit in order:
        own = (me >> bit) & 1
        axis = 1 if bit == 0 else 0
        got = partner(take(array, axis, 1 - own).astype(BF16), bit, devices)
        array = take(array, axis, own) + got.astype(F32)
    return array


def gather_parts(array, order, devices):
    me = lax.axis_index("row")
    for bit in reversed(order):
        own = (me >> bit) & 1
        array = joined(array, partner(array, bit, devices), own, 1 if bit == 0 else 0)
    return array


def block(skip, capacity, groups, mesh, live, exits, tokens, exit_gains, gate_weight, up_weight, down_weight):
    row_devices, col_devices = mesh.shape["row"], mesh.shape["col"]
    chips = col_devices // 2
    order = ring_order(chips)
    onward = [(order[i] * 2 + k, order[(i + 1) % chips] * 2 + k) for i in range(chips) for k in range(2)]
    across = [(i, i ^ 1) for i in range(col_devices)]
    bits = list(range(row_devices.bit_length() - 1))
    first, second = bits, bits[1:] + bits[:1]
    core = lax.axis_index("col") % 2
    row_me = lax.axis_index("row")
    width = tokens.shape[1]

    live_counts = live.astype(jnp.int32)
    before = jnp.stack([core, 1 - core]) * jnp.sum(live_counts, axis=1)[::-1]
    number = (jnp.cumsum(live_counts, axis=1) - 1 + before[:, None]).reshape(-1)
    slot = lax.iota(jnp.int32, 2 * capacity)
    slot = jnp.where(slot < capacity, slot + core * capacity, slot - core * capacity)
    chosen = (number[None, :] == slot[:, None] + skip) & live.reshape(-1)[None, :]
    pick = chosen.astype(BF16)
    packed = jnp.dot(pick, tokens, preferred_element_type=F32)
    packed_exit = jnp.sum(jnp.where(chosen, exits.reshape(-1)[None, :], 0), axis=1)
    gains = exit_gains[0][None, :]
    for e in range(1, exit_gains.shape[0]):
        gains = jnp.where((packed_exit == e)[:, None], exit_gains[e][None, :], gains)
    gained = (packed * gains).astype(BF16)
    squares = jnp.sum(packed * packed, axis=1)
    for bit in bits:
        squares = squares + partner(squares, bit, row_devices)
    own_scale = lax.rsqrt(squares / (width * row_devices) + 1e-05)[:, None]

    high = own_scale[:capacity].astype(BF16)
    low = (own_scale[:capacity] - high.astype(F32)).astype(BF16)
    lane = lax.iota(jnp.int32, LANES)[None, :]
    tail = jnp.where(lane == 0, high, jnp.where(lane == 1, low, jnp.zeros((), BF16)))
    moving = jnp.concatenate([gained[:capacity], tail], 1)
    rows, scales = [gained], [own_scale]
    for _ in range(chips - 1):
        moving = lax.ppermute(moving, "col", onward)
        pair = jnp.concatenate([moving, lax.ppermute(moving, "col", across)], 0)
        rows.append(pair[:, :width])
        scales.append(pair[:, width : width + 1].astype(F32) + pair[:, width + 1 : width + 2].astype(F32))

    sums = [None] * chips
    for group in groups:
        inputs = jnp.concatenate([rows[s] for s in group], 0)
        scale = jnp.concatenate([scales[s] for s in group], 0)
        for bit in bits[1:]:
            scale = take(scale, 0, (row_me >> bit) & 1)
        gate = jnp.dot(inputs, gate_weight, preferred_element_type=F32)
        gate = reduce_parts(gate, first, row_devices)
        up = jnp.dot(inputs, up_weight, preferred_element_type=F32)
        up = reduce_parts(up, second, row_devices)
        hidden = (jax.nn.silu(gate * scale) * (up * scale)).astype(BF16)
        half = hidden.shape[1]
        cut = (half // LANES + 1) // 2 * LANES
        left = gather_parts(hidden[:, :cut], first, row_devices)
        right = gather_parts(hidden[:, cut:], second, row_devices)
        rest = half - cut
        hidden = jnp.concatenate([left[:, :cut], right[:, :rest], left[:, cut:], right[:, rest:]], 1)
        part = jnp.dot(hidden, down_weight, preferred_element_type=F32)
        for i, s in enumerate(group):
            at = 2 * capacity * i
            mine, theirs = part[at : at + capacity], part[at + capacity : at + 2 * capacity]
            sums[s] = mine + lax.ppermute(theirs.astype(BF16), "col", across).astype(F32)

    total = sums[0]
    if chips > 1:
        carry = sums[1]
        for s in range(2, chips):
            carry = sums[s] + lax.ppermute(carry.astype(BF16), "col", onward).astype(F32)
        total = total + lax.ppermute(carry.astype(BF16), "col", onward).astype(F32)
    total = total.astype(BF16)
    total = jnp.concatenate([total, lax.ppermute(total, "col", across)], 0)
    return jnp.dot(pick[:, : tokens.shape[0] // 2].T, total, preferred_element_type=F32).astype(BF16)


def per_device(mesh, tokens, draft_counts, exit_layers, exit_gains, gate_weight, up_weight, down_weight):
    col_devices = mesh.shape["col"]
    chips = col_devices // 2
    local_rows = tokens.shape[0]
    me = lax.axis_index("col")
    tokens = jnp.concatenate([tokens, lax.ppermute(tokens, "col", [(i, i ^ 1) for i in range(col_devices)])], 0)

    most = jnp.max(jnp.sum(draft_counts.reshape(chips, -1), axis=1))
    sequences = local_rows // DRAFT

    def own(table):
        both = [lax.dynamic_slice_in_dim(table, d * sequences, sequences) for d in (me, me ^ 1)]
        return jnp.broadcast_to(jnp.stack(both)[:, :, None], (2, sequences, DRAFT)).reshape(2, local_rows)

    live = lax.iota(jnp.int32, local_rows)[None, :] % DRAFT < own(draft_counts)
    exits = own(exit_layers)
    capacity = local_rows * 3 // 4
    rest = local_rows - capacity
    operands = (live, exits, tokens, exit_gains, gate_weight, up_weight, down_weight)
    groups = [[s] for s in range(chips)] if chips < 4 else [[0], list(range(1, chips - 1)), [chips - 1]]
    out = block(0, capacity, groups, mesh, *operands)
    more = lax.cond(
        most > 2 * capacity,
        functools.partial(block, 2 * capacity, rest, [list(range(chips))], mesh),
        lambda *_: jnp.zeros((local_rows, tokens.shape[1]), BF16),
        *operands,
    )
    return out + more


def solution(mesh):
    return jax.shard_map(
        functools.partial(per_device, mesh),
        mesh=mesh,
        in_specs=(
            P("col", "row"),
            P(),
            P(),
            P(None, "row"),
            P("row", "col"),
            P("row", "col"),
            P("col", "row"),
        ),
        out_specs=P("col", "row"),
        check_vma=False,
    )
```

```python
import functools

import jax
import jax.numpy as jnp
from jax import lax
from jax.sharding import PartitionSpec as P

DRAFT = 4
LANES = 128
F32, BF16 = jnp.float32, jnp.bfloat16


def ring_order(chips):
    return [0] + list(range(1, chips, 2)) + list(range(chips - 2 + chips % 2, 0, -2))


def take(array, axis, part):
    size = array.shape[axis] // 2
    return lax.dynamic_slice_in_dim(array, part * size, size, axis)


def joined(mine, theirs, bit, axis):
    low = jnp.where(bit == 0, mine, theirs)
    high = jnp.where(bit == 0, theirs, mine)
    return jnp.concatenate([low, high], axis)


def partner(array, bit, devices):
    return lax.ppermute(array, "row", [(i, i ^ (1 << bit)) for i in range(devices)])


class Halving:
    def __init__(self, array, order, devices):
        self.array, self.order, self.devices = array, list(order), devices
        self.got = None

    def send(self):
        bit = self.order[0]
        own = (lax.axis_index("row") >> bit) & 1
        self.got = partner(take(self.array, 0 if bit else 1, 1 - own).astype(BF16), bit, self.devices)
        return self

    def add(self):
        bit = self.order.pop(0)
        own = (lax.axis_index("row") >> bit) & 1
        self.array = take(self.array, 0 if bit else 1, own) + self.got.astype(F32)
        self.got = None
        return self

    def finish(self):
        while self.order:
            if self.got is None:
                self.send()
            self.add()
        return self.array


class Gathering:
    def __init__(self, array, order, devices):
        self.array, self.order, self.devices = array, list(order), devices
        self.got = None

    def send(self):
        self.got = partner(self.array, self.order[-1], self.devices)
        return self

    def add(self):
        bit = self.order.pop()
        own = (lax.axis_index("row") >> bit) & 1
        self.array = joined(self.array, self.got, own, 0 if bit else 1)
        self.got = None
        return self

    def finish(self):
        while self.order:
            if self.got is None:
                self.send()
            self.add()
        return self.array


class Hidden:
    def __init__(self, devices, orders, gate, up, scale):
        me = lax.axis_index("row")
        for bit in sorted(b for b in orders[0] if b):
            scale = take(scale, 0, (me >> bit) & 1)
        hidden = (jax.nn.silu(gate * scale) * (up * scale)).astype(BF16)
        half = hidden.shape[1]
        cut = (half // LANES + 1) // 2 * LANES
        self.spans = [(0, half)] if len(orders) == 1 else [(0, cut), (cut, half)]
        self.pieces = [Gathering(hidden[:, lo:hi], order, devices) for (lo, hi), order in zip(self.spans, orders)]

    @property
    def got(self):
        return tuple(p.got for p in self.pieces)

    @got.setter
    def got(self, values):
        for p, v in zip(self.pieces, values):
            p.got = v

    def send(self):
        for p in self.pieces:
            p.send()
        return self

    def add(self):
        for p in self.pieces:
            p.add()
        return self

    def finish(self):
        wholes = [p.finish() for p in self.pieces]
        if len(wholes) == 1:
            return wholes[0]
        widths = [hi - lo for lo, hi in self.spans]
        return jnp.concatenate(
            [w[:, :n] for w, n in zip(wholes, widths)] + [w[:, n:] for w, n in zip(wholes, widths)], 1
        )


def tie(*values):
    return lax.optimization_barrier(values)


class Plan:
    def __init__(self, mesh, gate_weight, up_weight, down_weight):
        self.row_devices, col_devices = mesh.shape["row"], mesh.shape["col"]
        self.chips = col_devices // 2
        order = ring_order(self.chips)
        self.hops = [
            [(order[i] * 2 + k, order[(i + s) % self.chips] * 2 + k) for i in range(self.chips) for k in range(2)]
            for s in range(self.chips)
        ]
        self.other_core = [(i, i ^ 1) for i in range(col_devices)]
        self.bits = list(range(self.row_devices.bit_length() - 1))
        self.first, self.second = self.bits, self.bits[1:] + self.bits[:1]
        self.gate_weight, self.up_weight, self.down_weight = gate_weight, up_weight, down_weight

    def across(self, array):
        return lax.ppermute(array, "col", self.other_core)

    def onward(self, array, steps=1):
        return lax.ppermute(array, "col", self.hops[steps])

    def gate(self, rows):
        return jnp.dot(rows, self.gate_weight, preferred_element_type=F32)

    def up(self, rows):
        return jnp.dot(rows, self.up_weight, preferred_element_type=F32)

    def halve(self, array, order):
        return Halving(array, order, self.row_devices)

    def hidden(self, gate, up, scale, *orders):
        return Hidden(self.row_devices, orders, gate.finish(), up.finish(), scale)

    def down(self, hidden, part=slice(None)):
        return jnp.dot(hidden, self.down_weight[:, part], preferred_element_type=F32)

    def both_cores(self, part, capacity):
        part = part.reshape(-1, 2, capacity, part.shape[1])
        return list(part[:, 0] + self.across(part[:, 1].astype(BF16)).astype(F32))


def block(skip, capacity, staged, mesh, counts, exits, tokens, others, exit_gains, gate_weight, up_weight, down_weight):
    plan = Plan(mesh, gate_weight, up_weight, down_weight)
    chips = plan.chips
    core = lax.axis_index("col") % 2
    local_rows, width = tokens.shape

    sequences = counts.shape[0]
    place = lax.iota(jnp.int32, sequences)
    rank = (place + core * (sequences // 2)) % sequences
    start = jnp.sum(jnp.where(rank[None, :] < rank[:, None], counts[None, :], 0), axis=1)

    def pack(half):
        number = lax.iota(jnp.int32, capacity) + (skip + half * capacity)
        inside = (number[:, None] >= start[None, :]) & (number[:, None] < (start + counts)[None, :])
        row = jnp.sum(jnp.where(inside, number[:, None] + (DRAFT * place - start + 1)[None, :], 0), axis=1) - 1
        row_exit = jnp.sum(jnp.where(inside, exits[None, :], 0), axis=1)
        columns = lax.iota(jnp.int32, local_rows)[None, :]
        here = (row[:, None] == columns).astype(BF16)
        there = (row[:, None] == columns + local_rows).astype(BF16)
        packed = jnp.dot(here, tokens, preferred_element_type=F32) + jnp.dot(there, others, preferred_element_type=F32)
        gains = exit_gains[0][None, :]
        for e in range(1, exit_gains.shape[0]):
            gains = jnp.where((row_exit == e)[:, None], exit_gains[e][None, :], gains)
        return row, (packed * gains).astype(BF16), jnp.sum(packed * packed, axis=1)

    row, own_half, squares = pack(core)
    row_other, other_half, squares_other = pack(1 - core)
    squares = jnp.concatenate([squares, squares_other])

    def rows_of(steps, ring):
        pairs = []
        for s in steps:
            pairs += [own_half, other_half] if s == 0 else [ring[s], plan.across(ring[s])]
        return jnp.concatenate(pairs, 0)

    def all_scales(squares):
        own = lax.rsqrt(squares / (width * plan.row_devices) + 1e-05)
        return [own] + [plan.onward(own, s) for s in range(1, chips)]

    def scale_of(steps):
        return jnp.concatenate([scales[s] for s in steps])[:, None]

    ring = [own_half]
    first, second = plan.first, plan.second
    if not staged:
        for s in range(1, chips):
            ring.append(plan.onward(ring[-1]))
        for bit in plan.bits:
            squares = squares + partner(squares, bit, plan.row_devices)
        scales = all_scales(squares)
        steps = list(range(chips))
        rows = rows_of(steps, ring)
        gate, up = plan.halve(plan.gate(rows), first), plan.halve(plan.up(rows), second)
        hidden = plan.hidden(gate, up, scale_of(steps), first, second).finish()
        sums = plan.both_cores(plan.down(hidden), capacity)
        carry = None
        for s in range(1, chips):
            carry = plan.onward((sums[s] if carry is None else sums[s] + carry.astype(F32)).astype(BF16))
    else:
        low, mid, b, c = [0], list(range(1, chips - 2)), [chips - 2], [chips - 1]
        split, half = 2 * capacity, width // 2
        for s in mid:
            ring.append(plan.onward(ring[-1]))
        rows_low = rows_of(low, ring)
        gate_low = plan.gate(rows_low)
        ring[-1], rows_low, gate_low = tie(ring[-1], rows_low, gate_low)

        gate_low = plan.halve(gate_low, first).send()
        ring.append(plan.onward(ring[-1]))
        rows_mid = rows_of(mid, ring)
        gate_mid = plan.gate(rows_mid)
        ring[-1], rows_low, rows_mid, gate_low.got, squares, gate_mid = tie(
            ring[-1], rows_low, rows_mid, gate_low.got, squares, gate_mid
        )

        gate_mid = plan.halve(gate_mid, second).send()
        gate_low.add().send()
        ring.append(plan.onward(ring[-1]))
        rows_b = rows_of(b, ring)
        squares_got = partner(squares, 0, plan.row_devices)
        up_a = plan.up(jnp.concatenate([rows_low, rows_mid], 0))
        ring[-1], rows_b, gate_mid.got, squares_got, up_a = tie(ring[-1], rows_b, gate_mid.got, squares_got, up_a)

        up_low, up_mid = plan.halve(up_a[:split], first).send(), plan.halve(up_a[split:], second).send()
        gate_mid.add().send()
        squares = squares + squares_got
        squares_got = partner(squares, 1, plan.row_devices)
        gate_b = plan.gate(rows_b)
        rows_b, up_low.got, up_mid.got, gate_low.got, squares_got, gate_b = tie(
            rows_b, up_low.got, up_mid.got, gate_low.got, squares_got, gate_b
        )

        up_low.add().send()
        up_mid.add().send()
        gate_b = plan.halve(gate_b, first).send()
        squares = squares + squares_got
        for bit in plan.bits[2:]:
            squares = squares + partner(squares, bit, plan.row_devices)
        scales = all_scales(squares)
        rows_c = rows_of(c, ring)
        up_b = plan.up(rows_b)
        rows_c, up_low.got, up_mid.got, gate_mid.got, up_b, *scales = tie(
            rows_c, up_low.got, up_mid.got, gate_mid.got, up_b, *scales
        )

        hidden_low = plan.hidden(gate_low, up_low, scale_of(low), first).send()
        hidden_mid = plan.hidden(gate_mid, up_mid, scale_of(mid), second).send()
        up_b = plan.halve(up_b, second).send()
        gate_c = plan.gate(rows_c)
        rows_c, hidden_low.got, hidden_mid.got, gate_b.got, gate_c = tie(
            rows_c, hidden_low.got, hidden_mid.got, gate_b.got, gate_c
        )

        hidden_low.add().send()
        hidden_mid.add().send()
        gate_b.add().send()
        up_c = plan.up(rows_c)
        hidden_low.got, hidden_mid.got, up_b.got, gate_c, up_c = tie(
            hidden_low.got, hidden_mid.got, up_b.got, gate_c, up_c
        )

        up_b.add().send()
        up_c = plan.halve(up_c, second).send()
        gate_c = plan.halve(gate_c, first).send()
        hidden_a = jnp.concatenate([hidden_low.finish(), hidden_mid.finish()], 0)
        down_a = plan.down(hidden_a, slice(0, half))
        hidden_a, up_b.got, gate_b.got, down_a = tie(hidden_a, up_b.got, gate_b.got, down_a)

        hidden_b = plan.hidden(gate_b, up_b, scale_of(b), first, second).send()
        down_a = jnp.concatenate([down_a, plan.down(hidden_a, slice(half, width))], 1)
        hidden_b.got, gate_c.got, up_c.got, down_a = tie(hidden_b.got, gate_c.got, up_c.got, down_a)

        hidden_b.add().send()
        gate_c.add().send()
        up_c.add().send()
        sums = plan.both_cores(down_a, capacity)
        hidden_b, *sums = tie(hidden_b.finish(), *sums)

        carry = sums[1]
        for s in mid[1:]:
            carry = sums[s] + plan.onward(carry.astype(BF16)).astype(F32)
        carry = plan.onward(carry.astype(BF16))
        down_b = plan.down(hidden_b, slice(0, half))
        hidden_b, gate_c.got, up_c.got, down_b = tie(hidden_b, gate_c.got, up_c.got, down_b)

        hidden_c = plan.hidden(gate_c, up_c, scale_of(c), first, second).send()
        down_b = jnp.concatenate([down_b, plan.down(hidden_b, slice(half, width))], 1)
        hidden_c.got, carry, down_b = tie(hidden_c.got, carry, down_b)

        hidden_c.add().send()
        total = plan.both_cores(down_b, capacity)[0] + carry.astype(F32)
        carries = [plan.onward(total[:, :half].astype(BF16)), plan.onward(total[:, half:].astype(BF16))]
        hidden_c = hidden_c.finish()
        down_c = plan.down(hidden_c, slice(0, half))
        hidden_c, carries[0], down_c = tie(hidden_c, carries[0], down_c)

        total = plan.both_cores(down_c, capacity)[0] + carries[0].astype(F32)
        carries[0] = plan.onward(total.astype(BF16))
        total = plan.both_cores(plan.down(hidden_c, slice(half, width)), capacity)[0] + carries[1].astype(F32)
        carry = jnp.concatenate([carries[0], plan.onward(total.astype(BF16))], 1)

    total = sums[0] if carry is None else sums[0] + carry.astype(F32)
    total = total.astype(BF16)
    total = jnp.concatenate([total, plan.across(total)], 0)
    source = jnp.concatenate([row, row_other])
    pick = (lax.iota(jnp.int32, local_rows)[:, None] == source[None, :]).astype(BF16)
    return jnp.dot(pick, total, preferred_element_type=F32).astype(BF16)


def per_device(mesh, tokens, draft_counts, exit_layers, exit_gains, gate_weight, up_weight, down_weight):
    col_devices = mesh.shape["col"]
    chips = col_devices // 2
    local_rows = tokens.shape[0]
    me = lax.axis_index("col")
    others = lax.ppermute(tokens, "col", [(i, i ^ 1) for i in range(col_devices)])
    sequences = local_rows // DRAFT

    def own(table):
        return jnp.concatenate([lax.dynamic_slice_in_dim(table, d * sequences, sequences) for d in (me, me ^ 1)])

    capacity = local_rows * 3 // 4
    most = jnp.max(jnp.sum(draft_counts.reshape(chips, -1), axis=1))
    operands = (own(draft_counts), own(exit_layers), tokens, others, exit_gains, gate_weight, up_weight, down_weight)
    out = block(0, capacity, chips >= 4, mesh, *operands)
    return lax.cond(
        most > 2 * capacity,
        lambda done, *rest: done + block(2 * capacity, local_rows - capacity, False, mesh, *rest),
        lambda done, *rest: done,
        out,
        *operands,
    )


def solution(mesh):
    return jax.shard_map(
        functools.partial(per_device, mesh),
        mesh=mesh,
        in_specs=(
            P("col", "row"),
            P(),
            P(),
            P(None, "row"),
            P("row", "col"),
            P("row", "col"),
            P("col", "row"),
        ),
        out_specs=P("col", "row"),
        check_vma=False,
    )
```

```python
import functools

import jax
import jax.numpy as jnp
from jax import lax
from jax.sharding import PartitionSpec as P

DRAFT = 4
LANES = 128
F32, BF16 = jnp.float32, jnp.bfloat16


def ring_order(chips):
    return [0] + list(range(1, chips, 2)) + list(range(chips - 2 + chips % 2, 0, -2))


def take(array, axis, part):
    size = array.shape[axis] // 2
    return lax.dynamic_slice_in_dim(array, part * size, size, axis)


def joined(mine, theirs, bit, axis):
    low = jnp.where(bit == 0, mine, theirs)
    high = jnp.where(bit == 0, theirs, mine)
    return jnp.concatenate([low, high], axis)


def partner(array, bit, devices):
    return lax.ppermute(array, "row", [(i, i ^ (1 << bit)) for i in range(devices)])


class Halving:
    def __init__(self, array, order, devices):
        self.array, self.order, self.devices = array, list(order), devices
        self.got = None

    def send(self, pieces=1):
        bit = self.order[0]
        own = (lax.axis_index("row") >> bit) & 1
        payload = take(self.array, 0 if bit else 1, 1 - own).astype(BF16)
        parts = jnp.split(payload, pieces, 1 if bit else 0)
        self.got = tuple(partner(part, bit, self.devices) for part in parts)
        return self

    def add(self):
        bit = self.order.pop(0)
        own = (lax.axis_index("row") >> bit) & 1
        got = self.got[0] if len(self.got) == 1 else jnp.concatenate(self.got, 1 if bit else 0)
        self.array = take(self.array, 0 if bit else 1, own) + got.astype(F32)
        self.got = None
        return self

    def finish(self):
        while self.order:
            if self.got is None:
                self.send()
            self.add()
        return self.array


class Gathering:
    def __init__(self, array, order, devices):
        self.array, self.order, self.devices = array, list(order), devices
        self.got = None

    def send(self):
        self.got = partner(self.array, self.order[-1], self.devices)
        return self

    def add(self):
        bit = self.order.pop()
        own = (lax.axis_index("row") >> bit) & 1
        self.array = joined(self.array, self.got, own, 0 if bit else 1)
        self.got = None
        return self

    def finish(self):
        while self.order:
            if self.got is None:
                self.send()
            self.add()
        return self.array


class Hidden:
    def __init__(self, devices, orders, gate, up, scale):
        me = lax.axis_index("row")
        for bit in sorted(b for b in orders[0] if b):
            scale = take(scale, 0, (me >> bit) & 1)
        hidden = (jax.nn.silu(gate * scale) * (up * scale)).astype(BF16)
        half = hidden.shape[1]
        cut = (half // LANES + 1) // 2 * LANES
        self.spans = [(0, half)] if len(orders) == 1 else [(0, cut), (cut, half)]
        self.pieces = [Gathering(hidden[:, lo:hi], order, devices) for (lo, hi), order in zip(self.spans, orders)]

    @property
    def parts(self):
        return tuple(p.array for p in self.pieces)

    @parts.setter
    def parts(self, values):
        for p, v in zip(self.pieces, values):
            p.array = v

    @property
    def got(self):
        return tuple(p.got for p in self.pieces)

    @got.setter
    def got(self, values):
        for p, v in zip(self.pieces, values):
            p.got = v

    def send(self):
        for p in self.pieces:
            p.send()
        return self

    def add(self):
        for p in self.pieces:
            p.add()
        return self

    def finish(self):
        wholes = [p.finish() for p in self.pieces]
        if len(wholes) == 1:
            return wholes[0]
        widths = [hi - lo for lo, hi in self.spans]
        return jnp.concatenate(
            [w[:, :n] for w, n in zip(wholes, widths)] + [w[:, n:] for w, n in zip(wholes, widths)], 1
        )


def tie(*values):
    return lax.optimization_barrier(values)


class Plan:
    def __init__(self, mesh, gate_weight, up_weight, down_weight):
        self.row_devices, col_devices = mesh.shape["row"], mesh.shape["col"]
        self.chips = col_devices // 2
        order = ring_order(self.chips)
        self.hops = [
            [(order[i] * 2 + k, order[(i + s) % self.chips] * 2 + k) for i in range(self.chips) for k in range(2)]
            for s in range(self.chips)
        ]
        self.other_core = [(i, i ^ 1) for i in range(col_devices)]
        self.bits = list(range(self.row_devices.bit_length() - 1))
        self.first, self.second = self.bits, self.bits[1:] + self.bits[:1]
        self.gate_weight, self.up_weight, self.down_weight = gate_weight, up_weight, down_weight

    def across(self, array):
        return lax.ppermute(array, "col", self.other_core)

    def onward(self, array, steps=1):
        return lax.ppermute(array, "col", self.hops[steps])

    def gate(self, rows):
        return jnp.dot(rows, self.gate_weight, preferred_element_type=F32)

    def up(self, rows):
        return jnp.dot(rows, self.up_weight, preferred_element_type=F32)

    def halve(self, array, order):
        return Halving(array, order, self.row_devices)

    def hidden(self, gate, up, scale, *orders):
        return Hidden(self.row_devices, orders, gate.finish(), up.finish(), scale)

    def down(self, hidden, part=slice(None)):
        return jnp.dot(hidden, self.down_weight[:, part], preferred_element_type=F32)

    def both_cores(self, part, capacity):
        part = part.reshape(-1, 2, capacity, part.shape[1])
        return list(part[:, 0] + self.across(part[:, 1].astype(BF16)).astype(F32))


def block(skip, capacity, staged, mesh, most, counts, exits, tokens, others, exit_gains, gate_weight, up_weight, down_weight):
    plan = Plan(mesh, gate_weight, up_weight, down_weight)
    chips = plan.chips
    core = lax.axis_index("col") % 2
    local_rows, width = tokens.shape

    sequences = counts.shape[0]
    place = lax.iota(jnp.int32, sequences)
    rank = (place + core * (sequences // 2)) % sequences
    start = jnp.sum(jnp.where(rank[None, :] < rank[:, None], counts[None, :], 0), axis=1)

    def pack(half):
        number = lax.iota(jnp.int32, capacity) + (skip + half * capacity)
        inside = (number[:, None] >= start[None, :]) & (number[:, None] < (start + counts)[None, :])
        row = jnp.sum(jnp.where(inside, number[:, None] + (DRAFT * place - start + 1)[None, :], 0), axis=1) - 1
        row_exit = jnp.sum(jnp.where(inside, exits[None, :], 0), axis=1)
        columns = lax.iota(jnp.int32, local_rows)[None, :]
        here = (row[:, None] == columns).astype(BF16)
        there = (row[:, None] == columns + local_rows).astype(BF16)
        packed = jnp.dot(here, tokens, preferred_element_type=F32) + jnp.dot(there, others, preferred_element_type=F32)
        gains = exit_gains[0][None, :]
        for e in range(1, exit_gains.shape[0]):
            gains = jnp.where((row_exit == e)[:, None], exit_gains[e][None, :], gains)
        return row, (packed * gains).astype(BF16), jnp.sum(packed * packed, axis=1)

    row, own_half, squares = pack(core)
    row_other, other_half, squares_other = pack(1 - core)
    squares = jnp.concatenate([squares, squares_other])

    def rows_of(steps, ring):
        pairs = []
        for s in steps:
            pairs += [own_half, other_half] if s == 0 else [ring[s], plan.across(ring[s])]
        return jnp.concatenate(pairs, 0)

    def all_scales(squares):
        own = lax.rsqrt(squares / (width * plan.row_devices) + 1e-05)
        return [own] + [plan.onward(own, s) for s in range(1, chips)]

    def scale_of(steps):
        return jnp.concatenate([scales[s] for s in steps])[:, None]

    ring = [own_half]
    first, second = plan.first, plan.second
    if not staged:
        for s in range(1, chips):
            ring.append(plan.onward(ring[-1]))
        for bit in plan.bits:
            squares = squares + partner(squares, bit, plan.row_devices)
        scales = all_scales(squares)
        steps = list(range(chips))
        rows = rows_of(steps, ring)
        gate, up = plan.halve(plan.gate(rows), first), plan.halve(plan.up(rows), second)
        hidden = plan.hidden(gate, up, scale_of(steps), first, second).finish()
        sums = plan.both_cores(plan.down(hidden), capacity)
        carry = None
        for s in range(1, chips):
            carry = plan.onward((sums[s] if carry is None else sums[s] + carry.astype(F32)).astype(BF16))
    else:
        near, last = chips // 2, chips - 1
        low, mid, far, end = [0], list(range(1, near)), list(range(near, last)), [last]
        split, units = 2 * capacity, gate_weight.shape[1] // 2
        spans = (slice(0, width // 2), slice(width // 2, width))
        for s in mid:
            ring.append(plan.onward(ring[-1]))
        rows_low = rows_of(low, ring)
        squares_got = partner(squares, 0, plan.row_devices)
        gate_low = plan.gate(rows_low)
        ring[-1], rows_low, squares_got, gate_low = tie(ring[-1], rows_low, squares_got, gate_low)

        gate_low = plan.halve(gate_low, first).send()
        for s in far:
            ring.append(plan.onward(ring[-1]))
        squares = squares + squares_got
        squares_got = partner(squares, 1, plan.row_devices)
        rows_mid = rows_of(mid, ring)
        gate_mid = plan.gate(rows_mid)
        ring[-1], rows_low, rows_mid, gate_low.got, squares_got, gate_mid = tie(
            ring[-1], rows_low, rows_mid, gate_low.got, squares_got, gate_mid
        )

        gate_mid = plan.halve(gate_mid, second).send()
        gate_low.add().send()
        ring.append(plan.onward(ring[-1]))
        squares = squares + squares_got
        for bit in plan.bits[2:]:
            squares = squares + partner(squares, bit, plan.row_devices)
        scales = all_scales(squares)
        rows_far = rows_of(far, ring)
        up = plan.up(jnp.concatenate([rows_low, rows_mid], 0))
        ring[-1], rows_far, gate_mid.got, up, *scales = tie(ring[-1], rows_far, gate_mid.got, up, *scales)

        up_low, up_mid = plan.halve(up[:split], first).send(), plan.halve(up[split:], second).send()
        gate_mid.add().send()
        rows = jnp.concatenate([rows_far, rows_of(end, ring)], 0)
        split = rows_far.shape[0]
        gate = plan.gate(rows)
        rows, up_low.got, up_mid.got, gate_low.got, gate = tie(rows, up_low.got, up_mid.got, gate_low.got, gate)

        up_low.add().send()
        up_mid.add().send()
        gate_far, gate_end = plan.halve(gate[:split], first).send(2), plan.halve(gate[split:], second).send(2)
        up = jnp.dot(rows, up_weight[:, :units], preferred_element_type=F32)
        (far_0, far_1), (end_0, end_1) = gate_far.got, gate_end.got
        rows, up_low.got, up_mid.got, gate_mid.got, far_0, end_0, up = tie(
            rows, up_low.got, up_mid.got, gate_mid.got, far_0, end_0, up
        )
        gate_far.got, gate_end.got = (far_0, far_1), (end_0, end_1)

        hidden_low = plan.hidden(gate_low, up_low, scale_of(low), first).send()
        hidden_mid = plan.hidden(gate_mid, up_mid, scale_of(mid), second).send()
        up = jnp.concatenate([up, jnp.dot(rows, up_weight[:, units:], preferred_element_type=F32)], 1)
        hidden_low.got, hidden_mid.got, gate_far.got, gate_end.got, most, up = tie(
            hidden_low.got, hidden_mid.got, gate_far.got, gate_end.got, most, up
        )

        hidden_low.add().send()
        hidden_mid.add().send()
        up_far, up_end = plan.halve(up[:split], first).send(), plan.halve(up[split:], second).send()
        gate_far.add().send()
        gate_end.add().send()
        hidden = jnp.concatenate([hidden_low.finish(), hidden_mid.finish()], 0)
        down = plan.down(hidden, spans[0])
        hidden, up_far.got, up_end.got, down = tie(hidden, up_far.got, up_end.got, down)

        up_far.add().send()
        up_end.add().send()
        down = jnp.concatenate([down, plan.down(hidden, spans[1])], 1)
        up_far.got, up_end.got, gate_far.got, gate_end.got, down = tie(
            up_far.got, up_end.got, gate_far.got, gate_end.got, down
        )

        hidden_far = plan.hidden(gate_far, up_far, scale_of(far), first, second).send()
        hidden_end = plan.hidden(gate_end, up_end, scale_of(end), first, second)
        sums = plan.both_cores(down, capacity)
        hidden_far.got, hidden_end.parts, sums = tie(hidden_far.got, hidden_end.parts, sums)

        def passed(sums, carry=None):
            for total in sums:
                carry = plan.onward((total if carry is None else total + carry.astype(F32)).astype(BF16))
            return carry

        hidden_far.add().send()
        hidden_end.send()
        carry = passed(sums[1:])
        hidden_far.got, hidden_end.got = tie(hidden_far.got, hidden_end.got)

        hidden_end.add().send()
        down = plan.down(hidden_far.finish())
        hidden_end.got, carry, down = tie(hidden_end.got, carry, down)

        hidden, sums_far = tie(hidden_end.finish(), plan.both_cores(down, capacity))
        carry = passed(sums_far, carry)
        down = plan.down(hidden)
        carry, down = tie(carry, down)
        carry = passed(plan.both_cores(down, capacity), carry)

    total = sums[0] if carry is None else sums[0] + carry.astype(F32)
    total = total.astype(BF16)
    total = jnp.concatenate([total, plan.across(total)], 0)
    source = jnp.concatenate([row, row_other])
    pick = (lax.iota(jnp.int32, local_rows)[:, None] == source[None, :]).astype(BF16)
    return most, jnp.dot(pick, total, preferred_element_type=F32).astype(BF16)


def per_device(mesh, tokens, draft_counts, exit_layers, exit_gains, gate_weight, up_weight, down_weight):
    col_devices = mesh.shape["col"]
    chips = col_devices // 2
    local_rows = tokens.shape[0]
    sequences = local_rows // DRAFT
    capacity = local_rows * 3 // 4

    def run(most, skip, capacity, staged):
        me = lax.axis_index("col")
        others = lax.ppermute(tokens, "col", [(i, i ^ 1) for i in range(col_devices)])
        table = draft_counts * exit_gains.shape[0] + exit_layers
        table = jnp.concatenate([lax.dynamic_slice_in_dim(table, d * sequences, sequences) for d in (me, me ^ 1)])
        counts, exits = table // exit_gains.shape[0], table % exit_gains.shape[0]
        return block(
            skip, capacity, staged, mesh, most, counts, exits, tokens, others,
            exit_gains, gate_weight, up_weight, down_weight,
        )

    most = jnp.max(jnp.sum(draft_counts.reshape(chips, -1), axis=1))
    most, out = run(most, 0, capacity, chips >= 4)
    return lax.cond(
        most > 2 * capacity,
        lambda done: done + run(most, 2 * capacity, local_rows - capacity, False)[1],
        lambda done: done,
        out,
    )


def solution(mesh):
    return jax.shard_map(
        functools.partial(per_device, mesh),
        mesh=mesh,
        in_specs=(
            P("col", "row"),
            P(),
            P(),
            P(None, "row"),
            P("row", "col"),
            P("row", "col"),
            P("col", "row"),
        ),
        out_specs=P("col", "row"),
        check_vma=False,
    )
```

```python
import functools

import jax
import jax.numpy as jnp
from jax import lax
from jax.sharding import PartitionSpec as P

DRAFT = 4
LANES = 128
F32, BF16 = jnp.float32, jnp.bfloat16


def ring_order(chips):
    return [0] + list(range(1, chips, 2)) + list(range(chips - 2 + chips % 2, 0, -2))


def take(array, axis, part):
    size = array.shape[axis] // 2
    return lax.dynamic_slice_in_dim(array, part * size, size, axis)


def joined(mine, theirs, bit, axis):
    low = jnp.where(bit == 0, mine, theirs)
    high = jnp.where(bit == 0, theirs, mine)
    return jnp.concatenate([low, high], axis)


def partner(array, bit, devices):
    return lax.ppermute(array, "row", [(i, i ^ (1 << bit)) for i in range(devices)])


class Halving:
    def __init__(self, array, order, devices):
        self.array, self.order, self.devices = array, list(order), devices
        self.got = None

    def send(self, pieces=1):
        bit = self.order[0]
        own = (lax.axis_index("row") >> bit) & 1
        payload = take(self.array, 0 if bit else 1, 1 - own).astype(BF16)
        parts = jnp.split(payload, pieces, 1 if bit else 0)
        self.got = tuple(partner(part, bit, self.devices) for part in parts)
        return self

    def add(self):
        bit = self.order.pop(0)
        own = (lax.axis_index("row") >> bit) & 1
        got = self.got[0] if len(self.got) == 1 else jnp.concatenate(self.got, 1 if bit else 0)
        self.array = take(self.array, 0 if bit else 1, own) + got.astype(F32)
        self.got = None
        return self

    def finish(self):
        while self.order:
            if self.got is None:
                self.send()
            self.add()
        return self.array


class Gathering:
    def __init__(self, array, order, devices):
        self.array, self.order, self.devices = array, list(order), devices
        self.got = None

    def send(self):
        self.got = partner(self.array, self.order[-1], self.devices)
        return self

    def add(self):
        bit = self.order.pop()
        own = (lax.axis_index("row") >> bit) & 1
        self.array = joined(self.array, self.got, own, 0 if bit else 1)
        self.got = None
        return self

    def finish(self):
        while self.order:
            if self.got is None:
                self.send()
            self.add()
        return self.array


class Hidden:
    def __init__(self, devices, orders, gate, up, scale):
        me = lax.axis_index("row")
        for bit in sorted(b for b in orders[0] if b):
            scale = take(scale, 0, (me >> bit) & 1)
        hidden = (jax.nn.silu(gate * scale) * (up * scale)).astype(BF16)
        half = hidden.shape[1]
        cut = (half // LANES + 1) // 2 * LANES
        self.spans = [(0, half)] if len(orders) == 1 else [(0, cut), (cut, half)]
        self.pieces = [Gathering(hidden[:, lo:hi], order, devices) for (lo, hi), order in zip(self.spans, orders)]

    @property
    def parts(self):
        return tuple(p.array for p in self.pieces)

    @parts.setter
    def parts(self, values):
        for p, v in zip(self.pieces, values):
            p.array = v

    @property
    def got(self):
        return tuple(p.got for p in self.pieces)

    @got.setter
    def got(self, values):
        for p, v in zip(self.pieces, values):
            p.got = v

    def send(self):
        for p in self.pieces:
            p.send()
        return self

    def add(self):
        for p in self.pieces:
            p.add()
        return self

    def finish(self):
        wholes = [p.finish() for p in self.pieces]
        if len(wholes) == 1:
            return wholes[0]
        widths = [hi - lo for lo, hi in self.spans]
        return jnp.concatenate(
            [w[:, :n] for w, n in zip(wholes, widths)] + [w[:, n:] for w, n in zip(wholes, widths)], 1
        )


def tie(*values):
    return lax.optimization_barrier(values)


class Plan:
    def __init__(self, mesh, gate_weight, up_weight, down_weight):
        self.row_devices, col_devices = mesh.shape["row"], mesh.shape["col"]
        self.chips = col_devices // 2
        order = ring_order(self.chips)
        self.hops = [
            [(order[i] * 2 + k, order[(i + s) % self.chips] * 2 + k) for i in range(self.chips) for k in range(2)]
            for s in range(self.chips)
        ]
        self.other_core = [(i, i ^ 1) for i in range(col_devices)]
        self.bits = list(range(self.row_devices.bit_length() - 1))
        self.first, self.second = self.bits, self.bits[1:] + self.bits[:1]
        self.gate_weight, self.up_weight, self.down_weight = gate_weight, up_weight, down_weight

    def across(self, array):
        return lax.ppermute(array, "col", self.other_core)

    def onward(self, array, steps=1):
        return lax.ppermute(array, "col", self.hops[steps])

    def gate(self, rows):
        return jnp.dot(rows, self.gate_weight, preferred_element_type=F32)

    def up(self, rows):
        return jnp.dot(rows, self.up_weight, preferred_element_type=F32)

    def halve(self, array, order):
        return Halving(array, order, self.row_devices)

    def hidden(self, gate, up, scale, *orders):
        return Hidden(self.row_devices, orders, gate.finish(), up.finish(), scale)

    def down(self, hidden, part=slice(None)):
        return jnp.dot(hidden, self.down_weight[:, part], preferred_element_type=F32)

    def both_cores(self, part, capacity):
        part = part.reshape(-1, 2, capacity, part.shape[1])
        return list(part[:, 0] + self.across(part[:, 1].astype(BF16)).astype(F32))


def block(skip, capacity, staged, mesh, most, counts, exits, tokens, others, exit_gains, gate_weight, up_weight, down_weight):
    plan = Plan(mesh, gate_weight, up_weight, down_weight)
    chips = plan.chips
    core = lax.axis_index("col") % 2
    local_rows, width = tokens.shape

    sequences = counts.shape[0]
    place = lax.iota(jnp.int32, sequences)
    rank = (place + core * (sequences // 2)) % sequences
    start = jnp.sum(jnp.where(rank[None, :] < rank[:, None], counts[None, :], 0), axis=1)

    def pack(half):
        number = lax.iota(jnp.int32, capacity) + (skip + half * capacity)
        inside = (number[:, None] >= start[None, :]) & (number[:, None] < (start + counts)[None, :])
        row = jnp.sum(jnp.where(inside, number[:, None] + (DRAFT * place - start + 1)[None, :], 0), axis=1) - 1
        row_exit = jnp.sum(jnp.where(inside, exits[None, :], 0), axis=1)
        columns = lax.iota(jnp.int32, local_rows)[None, :]
        here = (row[:, None] == columns).astype(BF16)
        there = (row[:, None] == columns + local_rows).astype(BF16)
        packed = jnp.dot(here, tokens, preferred_element_type=F32) + jnp.dot(there, others, preferred_element_type=F32)
        gains = exit_gains[0][None, :]
        for e in range(1, exit_gains.shape[0]):
            gains = jnp.where((row_exit == e)[:, None], exit_gains[e][None, :], gains)
        return row, (packed * gains).astype(BF16), jnp.sum(packed * packed, axis=1)

    row, own_half, squares = pack(core)
    row_other, other_half, squares_other = pack(1 - core)
    squares = jnp.concatenate([squares, squares_other])

    def rows_of(steps, ring):
        pairs = []
        for s in steps:
            pairs += [own_half, other_half] if s == 0 else [ring[s], plan.across(ring[s])]
        return jnp.concatenate(pairs, 0)

    def all_scales(squares):
        own = lax.rsqrt(squares / (width * plan.row_devices) + 1e-05)
        return [own] + [plan.onward(own, s) for s in range(1, chips)]

    def scale_of(steps):
        return jnp.concatenate([scales[s] for s in steps])[:, None]

    ring = [own_half]
    first, second = plan.first, plan.second
    if not staged:
        for s in range(1, chips):
            ring.append(plan.onward(ring[-1]))
        for bit in plan.bits:
            squares = squares + partner(squares, bit, plan.row_devices)
        scales = all_scales(squares)
        steps = list(range(chips))
        rows = rows_of(steps, ring)
        gate, up = plan.halve(plan.gate(rows), first), plan.halve(plan.up(rows), second)
        hidden = plan.hidden(gate, up, scale_of(steps), first, second).finish()
        sums = plan.both_cores(plan.down(hidden), capacity)
        carry = None
        for s in range(1, chips):
            carry = plan.onward((sums[s] if carry is None else sums[s] + carry.astype(F32)).astype(BF16))
    else:
        near, last = chips // 2, chips - 1
        low, mid, far, end = [0], list(range(1, near)), list(range(near, last)), [last]
        split, units = 2 * capacity, gate_weight.shape[1] // 2
        spans = (slice(0, width // 2), slice(width // 2, width))
        for s in mid:
            ring.append(plan.onward(ring[-1]))
        rows_low = rows_of(low, ring)
        squares_got = partner(squares, 0, plan.row_devices)
        gate_low = plan.gate(rows_low)
        ring[-1], rows_low, squares_got, gate_low = tie(ring[-1], rows_low, squares_got, gate_low)

        gate_low = plan.halve(gate_low, first).send()
        for s in far:
            ring.append(plan.onward(ring[-1]))
        squares = squares + squares_got
        squares_got = partner(squares, 1, plan.row_devices)
        rows_mid = rows_of(mid, ring)
        gate_mid = plan.gate(rows_mid)
        ring[-1], rows_low, rows_mid, gate_low.got, squares_got, gate_mid = tie(
            ring[-1], rows_low, rows_mid, gate_low.got, squares_got, gate_mid
        )

        gate_mid = plan.halve(gate_mid, second).send()
        gate_low.add().send()
        ring.append(plan.onward(ring[-1]))
        squares = squares + squares_got
        for bit in plan.bits[2:]:
            squares = squares + partner(squares, bit, plan.row_devices)
        scales = all_scales(squares)
        rows_far = rows_of(far, ring)
        up = plan.up(jnp.concatenate([rows_low, rows_mid], 0))
        ring[-1], rows_far, gate_mid.got, up, *scales = tie(ring[-1], rows_far, gate_mid.got, up, *scales)

        up_low, up_mid = plan.halve(up[:split], first).send(), plan.halve(up[split:], second).send()
        gate_mid.add().send()
        rows = jnp.concatenate([rows_far, rows_of(end, ring)], 0)
        split = rows_far.shape[0]
        gate = plan.gate(rows)
        rows, up_low.got, up_mid.got, gate_low.got, gate = tie(rows, up_low.got, up_mid.got, gate_low.got, gate)

        up_low.add().send()
        up_mid.add().send()
        gate_far, gate_end = plan.halve(gate[:split], first).send(2), plan.halve(gate[split:], second).send(2)
        up = jnp.dot(rows, up_weight[:, :units], preferred_element_type=F32)
        (far_0, far_1), (end_0, end_1) = gate_far.got, gate_end.got
        rows, up_low.got, up_mid.got, gate_mid.got, far_0, end_0, up = tie(
            rows, up_low.got, up_mid.got, gate_mid.got, far_0, end_0, up
        )
        gate_far.got, gate_end.got = (far_0, far_1), (end_0, end_1)

        hidden_low = plan.hidden(gate_low, up_low, scale_of(low), first).send()
        hidden_mid = plan.hidden(gate_mid, up_mid, scale_of(mid), second).send()
        cut = units + (units // LANES + 1) // 2 * LANES
        middle = jnp.dot(rows, up_weight[:, units:cut], preferred_element_type=F32)
        rows, hidden_low.got, hidden_mid.got, middle = tie(rows, hidden_low.got, hidden_mid.got, middle)

        hidden_low.add().send()
        hidden_mid.add().send()
        up = jnp.concatenate([up, middle, jnp.dot(rows, up_weight[:, cut:], preferred_element_type=F32)], 1)
        up_far, up_end = plan.halve(up[:split], first).send(), plan.halve(up[split:], second).send()
        hidden_low.got, hidden_mid.got, gate_far.got, gate_end.got, most, up_far.array, up_end.array = tie(
            hidden_low.got, hidden_mid.got, gate_far.got, gate_end.got, most, up_far.array, up_end.array
        )

        gate_far.add().send()
        gate_end.add().send()
        hidden = jnp.concatenate([hidden_low.finish(), hidden_mid.finish()], 0)
        down = plan.down(hidden, spans[0])
        hidden, up_far.got, up_end.got, down = tie(hidden, up_far.got, up_end.got, down)

        up_far.add().send()
        up_end.add().send()
        down = jnp.concatenate([down, plan.down(hidden, spans[1])], 1)
        up_far.got, up_end.got, gate_far.got, gate_end.got, down = tie(
            up_far.got, up_end.got, gate_far.got, gate_end.got, down
        )

        hidden_far = plan.hidden(gate_far, up_far, scale_of(far), first, second).send()
        hidden_end = plan.hidden(gate_end, up_end, scale_of(end), first, second)
        sums = plan.both_cores(down, capacity)
        hidden_far.got, hidden_end.parts, sums = tie(hidden_far.got, hidden_end.parts, sums)

        def passed(sums, carry=None):
            for total in sums:
                carry = plan.onward((total if carry is None else total + carry.astype(F32)).astype(BF16))
            return carry

        hidden_far.add().send()
        hidden_end.send()
        carry = passed(sums[1:])
        hidden_far.got, hidden_end.got = tie(hidden_far.got, hidden_end.got)

        hidden_end.add().send()
        down = plan.down(hidden_far.finish())
        hidden_end.got, carry, down = tie(hidden_end.got, carry, down)

        hidden, sums_far = tie(hidden_end.finish(), plan.both_cores(down, capacity))
        carry = passed(sums_far, carry)
        down = plan.down(hidden)
        carry, down = tie(carry, down)
        carry = passed(plan.both_cores(down, capacity), carry)

    total = sums[0] if carry is None else sums[0] + carry.astype(F32)
    total = total.astype(BF16)
    total = jnp.concatenate([total, plan.across(total)], 0)
    source = jnp.concatenate([row, row_other])
    pick = (lax.iota(jnp.int32, local_rows)[:, None] == source[None, :]).astype(BF16)
    return most, jnp.dot(pick, total, preferred_element_type=F32).astype(BF16)


def per_device(mesh, tokens, draft_counts, exit_layers, exit_gains, gate_weight, up_weight, down_weight):
    col_devices = mesh.shape["col"]
    chips = col_devices // 2
    local_rows = tokens.shape[0]
    sequences = local_rows // DRAFT
    capacity = local_rows * 3 // 4

    def run(most, skip, capacity, staged):
        me = lax.axis_index("col")
        others = lax.ppermute(tokens, "col", [(i, i ^ 1) for i in range(col_devices)])
        table = draft_counts * exit_gains.shape[0] + exit_layers
        table = jnp.concatenate([lax.dynamic_slice_in_dim(table, d * sequences, sequences) for d in (me, me ^ 1)])
        counts, exits = table // exit_gains.shape[0], table % exit_gains.shape[0]
        return block(
            skip, capacity, staged, mesh, most, counts, exits, tokens, others,
            exit_gains, gate_weight, up_weight, down_weight,
        )

    most = jnp.max(jnp.sum(draft_counts.reshape(chips, -1), axis=1))
    most, out = run(most, 0, capacity, chips >= 4)
    return lax.cond(
        most > 2 * capacity,
        lambda done: done + run(most, 2 * capacity, local_rows - capacity, False)[1],
        lambda done: done,
        out,
    )


def solution(mesh):
    return jax.shard_map(
        functools.partial(per_device, mesh),
        mesh=mesh,
        in_specs=(
            P("col", "row"),
            P(),
            P(),
            P(None, "row"),
            P("row", "col"),
            P("row", "col"),
            P("col", "row"),
        ),
        out_specs=P("col", "row"),
        check_vma=False,
    )
```

```python
import functools

import jax
import jax.numpy as jnp
from jax import lax
from jax.sharding import PartitionSpec as P

DRAFT = 4
LANES = 128
F32, BF16 = jnp.float32, jnp.bfloat16


def ring_order(chips):
    return [0] + list(range(1, chips, 2)) + list(range(chips - 2 + chips % 2, 0, -2))


def take(array, axis, part):
    size = array.shape[axis] // 2
    return lax.dynamic_slice_in_dim(array, part * size, size, axis)


def joined(mine, theirs, bit, axis):
    low = jnp.where(bit == 0, mine, theirs)
    high = jnp.where(bit == 0, theirs, mine)
    return jnp.concatenate([low, high], axis)


def partner(array, bit, devices):
    return lax.ppermute(array, "row", [(i, i ^ (1 << bit)) for i in range(devices)])


class Halving:
    def __init__(self, array, order, devices):
        self.array, self.order, self.devices = array, list(order), devices
        self.got = None

    def send(self, pieces=1):
        bit = self.order[0]
        own = (lax.axis_index("row") >> bit) & 1
        payload = take(self.array, 0 if bit else 1, 1 - own).astype(BF16)
        parts = jnp.split(payload, pieces, 1 if bit else 0)
        self.got = tuple(partner(part, bit, self.devices) for part in parts)
        return self

    def add(self):
        bit = self.order.pop(0)
        own = (lax.axis_index("row") >> bit) & 1
        got = self.got[0] if len(self.got) == 1 else jnp.concatenate(self.got, 1 if bit else 0)
        self.array = take(self.array, 0 if bit else 1, own) + got.astype(F32)
        self.got = None
        return self

    def finish(self):
        while self.order:
            if self.got is None:
                self.send()
            self.add()
        return self.array


class Gathering:
    def __init__(self, array, order, devices):
        self.array, self.order, self.devices = array, list(order), devices
        self.got = None

    def send(self):
        self.got = partner(self.array, self.order[-1], self.devices)
        return self

    def add(self):
        bit = self.order.pop()
        own = (lax.axis_index("row") >> bit) & 1
        self.array = joined(self.array, self.got, own, 0 if bit else 1)
        self.got = None
        return self

    def finish(self):
        while self.order:
            if self.got is None:
                self.send()
            self.add()
        return self.array


class Hidden:
    def __init__(self, devices, orders, gate, up, scale):
        me = lax.axis_index("row")
        for bit in sorted(b for b in orders[0] if b):
            scale = take(scale, 0, (me >> bit) & 1)
        hidden = (jax.nn.silu(gate * scale) * (up * scale)).astype(BF16)
        half = hidden.shape[1]
        cut = (half // LANES + 1) // 2 * LANES
        self.spans = [(0, half)] if len(orders) == 1 else [(0, cut), (cut, half)]
        self.pieces = [Gathering(hidden[:, lo:hi], order, devices) for (lo, hi), order in zip(self.spans, orders)]

    @property
    def parts(self):
        return tuple(p.array for p in self.pieces)

    @parts.setter
    def parts(self, values):
        for p, v in zip(self.pieces, values):
            p.array = v

    @property
    def got(self):
        return tuple(p.got for p in self.pieces)

    @got.setter
    def got(self, values):
        for p, v in zip(self.pieces, values):
            p.got = v

    def send(self):
        for p in self.pieces:
            p.send()
        return self

    def add(self):
        for p in self.pieces:
            p.add()
        return self

    def finish(self):
        wholes = [p.finish() for p in self.pieces]
        if len(wholes) == 1:
            return wholes[0]
        widths = [hi - lo for lo, hi in self.spans]
        return jnp.concatenate(
            [w[:, :n] for w, n in zip(wholes, widths)] + [w[:, n:] for w, n in zip(wholes, widths)], 1
        )


def tie(*values):
    return lax.optimization_barrier(values)


class Plan:
    def __init__(self, mesh, gate_weight, up_weight, down_weight):
        self.row_devices, col_devices = mesh.shape["row"], mesh.shape["col"]
        self.chips = col_devices // 2
        order = ring_order(self.chips)
        self.hops = [
            [(order[i] * 2 + k, order[(i + s) % self.chips] * 2 + k) for i in range(self.chips) for k in range(2)]
            for s in range(self.chips)
        ]
        self.other_core = [(i, i ^ 1) for i in range(col_devices)]
        self.bits = list(range(self.row_devices.bit_length() - 1))
        self.first, self.second = self.bits, self.bits[1:] + self.bits[:1]
        self.gate_weight, self.up_weight, self.down_weight = gate_weight, up_weight, down_weight

    def across(self, array):
        return lax.ppermute(array, "col", self.other_core)

    def onward(self, array, steps=1):
        return lax.ppermute(array, "col", self.hops[steps])

    def gate(self, rows):
        return jnp.dot(rows, self.gate_weight, preferred_element_type=F32)

    def up(self, rows):
        return jnp.dot(rows, self.up_weight, preferred_element_type=F32)

    def halve(self, array, order):
        return Halving(array, order, self.row_devices)

    def hidden(self, gate, up, scale, *orders):
        return Hidden(self.row_devices, orders, gate.finish(), up.finish(), scale)

    def down(self, hidden, part=slice(None)):
        return jnp.dot(hidden, self.down_weight[:, part], preferred_element_type=F32)

    def both_cores(self, part, capacity):
        mine, theirs = self.by_core(part, capacity)
        return list(mine + self.across(theirs.astype(BF16)).astype(F32))

    def by_core(self, part, capacity):
        part = part.reshape(-1, 2, capacity, part.shape[1])
        return part[:, 0], part[:, 1]


def block(skip, capacity, staged, mesh, most, counts, exits, tokens, others, exit_gains, gate_weight, up_weight, down_weight):
    plan = Plan(mesh, gate_weight, up_weight, down_weight)
    chips = plan.chips
    core = lax.axis_index("col") % 2
    local_rows, width = tokens.shape

    sequences = counts.shape[0]
    place = lax.iota(jnp.int32, sequences)
    rank = (place + core * (sequences // 2)) % sequences
    start = jnp.sum(jnp.where(rank[None, :] < rank[:, None], counts[None, :], 0), axis=1)

    def pack(half):
        number = lax.iota(jnp.int32, capacity) + (skip + half * capacity)
        inside = (number[:, None] >= start[None, :]) & (number[:, None] < (start + counts)[None, :])
        row = jnp.sum(jnp.where(inside, number[:, None] + (DRAFT * place - start + 1)[None, :], 0), axis=1) - 1
        row_exit = jnp.sum(jnp.where(inside, exits[None, :], 0), axis=1)
        columns = lax.iota(jnp.int32, local_rows)[None, :]
        here = (row[:, None] == columns).astype(BF16)
        there = (row[:, None] == columns + local_rows).astype(BF16)
        packed = jnp.dot(here, tokens, preferred_element_type=F32) + jnp.dot(there, others, preferred_element_type=F32)
        gains = exit_gains[0][None, :]
        for e in range(1, exit_gains.shape[0]):
            gains = jnp.where((row_exit == e)[:, None], exit_gains[e][None, :], gains)
        return row, (packed * gains).astype(BF16), jnp.sum(packed * packed, axis=1)

    row, own_half, squares = pack(core)
    row_other, other_half, squares_other = pack(1 - core)
    squares = jnp.concatenate([squares, squares_other])

    def rows_of(steps, ring):
        pairs = []
        for s in steps:
            pairs += [own_half, other_half] if s == 0 else [ring[s], plan.across(ring[s])]
        return jnp.concatenate(pairs, 0)

    def all_scales(squares):
        own = lax.rsqrt(squares / (width * plan.row_devices) + 1e-05)
        return [own] + [plan.onward(own, s) for s in range(1, chips)]

    def scale_of(steps):
        return jnp.concatenate([scales[s] for s in steps])[:, None]

    ring = [own_half]
    first, second = plan.first, plan.second
    if not staged:
        for s in range(1, chips):
            ring.append(plan.onward(ring[-1]))
        for bit in plan.bits:
            squares = squares + partner(squares, bit, plan.row_devices)
        scales = all_scales(squares)
        steps = list(range(chips))
        rows = rows_of(steps, ring)
        gate, up = plan.halve(plan.gate(rows), first), plan.halve(plan.up(rows), second)
        hidden = plan.hidden(gate, up, scale_of(steps), first, second).finish()
        sums = plan.both_cores(plan.down(hidden), capacity)
        carry = None
        for s in range(1, chips):
            carry = plan.onward((sums[s] if carry is None else sums[s] + carry.astype(F32)).astype(BF16))
    else:
        near, last = chips // 2, chips - 1
        low, mid, far, end = [0], list(range(1, near)), list(range(near, last)), [last]
        split, units = 2 * capacity, gate_weight.shape[1] // 2
        spans = (slice(0, width // 2), slice(width // 2, width))
        for s in mid:
            ring.append(plan.onward(ring[-1]))
        rows_low = rows_of(low, ring)
        squares_got = partner(squares, 0, plan.row_devices)
        gate_low = plan.gate(rows_low)
        ring[-1], rows_low, squares_got, gate_low = tie(ring[-1], rows_low, squares_got, gate_low)

        gate_low = plan.halve(gate_low, first).send()
        for s in far:
            ring.append(plan.onward(ring[-1]))
        squares = squares + squares_got
        squares_got = partner(squares, 1, plan.row_devices)
        rows_mid = rows_of(mid, ring)
        gate_mid = plan.gate(rows_mid)
        ring[-1], rows_low, rows_mid, gate_low.got, squares_got, gate_mid = tie(
            ring[-1], rows_low, rows_mid, gate_low.got, squares_got, gate_mid
        )

        gate_mid = plan.halve(gate_mid, second).send()
        gate_low.add().send()
        ring.append(plan.onward(ring[-1]))
        squares = squares + squares_got
        for bit in plan.bits[2:]:
            squares = squares + partner(squares, bit, plan.row_devices)
        scales = all_scales(squares)
        rows_far = rows_of(far, ring)
        up = plan.up(jnp.concatenate([rows_low, rows_mid], 0))
        ring[-1], rows_far, gate_mid.got, up, *scales = tie(ring[-1], rows_far, gate_mid.got, up, *scales)

        up_low, up_mid = plan.halve(up[:split], first).send(), plan.halve(up[split:], second).send()
        gate_mid.add().send()
        rows = jnp.concatenate([rows_far, rows_of(end, ring)], 0)
        split = rows_far.shape[0]
        gate = plan.gate(rows)
        rows, up_low.got, up_mid.got, gate_low.got, gate = tie(rows, up_low.got, up_mid.got, gate_low.got, gate)

        up_low.add().send()
        up_mid.add().send()
        gate_far, gate_end = plan.halve(gate[:split], first).send(2), plan.halve(gate[split:], second).send(2)
        up = jnp.dot(rows, up_weight[:, :units], preferred_element_type=F32)
        (far_0, far_1), (end_0, end_1) = gate_far.got, gate_end.got
        rows, up_low.got, up_mid.got, gate_mid.got, far_0, end_0, up = tie(
            rows, up_low.got, up_mid.got, gate_mid.got, far_0, end_0, up
        )
        gate_far.got, gate_end.got = (far_0, far_1), (end_0, end_1)

        hidden_low = plan.hidden(gate_low, up_low, scale_of(low), first).send()
        hidden_mid = plan.hidden(gate_mid, up_mid, scale_of(mid), second).send()
        cut = units + (units // LANES + 1) // 2 * LANES
        middle = jnp.dot(rows, up_weight[:, units:cut], preferred_element_type=F32)
        rows, hidden_low.got, hidden_mid.got, middle = tie(rows, hidden_low.got, hidden_mid.got, middle)

        hidden_low.add().send()
        hidden_mid.add().send()
        up = jnp.concatenate([up, middle, jnp.dot(rows, up_weight[:, cut:], preferred_element_type=F32)], 1)
        up_far, up_end = plan.halve(up[:split], first).send(), plan.halve(up[split:], second).send()
        hidden_low.got, hidden_mid.got, gate_far.got, gate_end.got, most, up_far.array, up_end.array = tie(
            hidden_low.got, hidden_mid.got, gate_far.got, gate_end.got, most, up_far.array, up_end.array
        )

        gate_far.add().send()
        gate_end.add().send()
        hidden = jnp.concatenate([hidden_low.finish(), hidden_mid.finish()], 0)
        down = plan.down(hidden, spans[0])
        hidden, up_far.got, up_end.got, down = tie(hidden, up_far.got, up_end.got, down)

        up_far.add().send()
        up_end.add().send()
        down = jnp.concatenate([down, plan.down(hidden, spans[1])], 1)
        up_far.got, up_end.got, gate_far.got, gate_end.got, down = tie(
            up_far.got, up_end.got, gate_far.got, gate_end.got, down
        )

        hidden_far = plan.hidden(gate_far, up_far, scale_of(far), first, second).send()
        hidden_end = plan.hidden(gate_end, up_end, scale_of(end), first, second)
        sums = plan.both_cores(down, capacity)
        hidden_far.got, hidden_end.parts, sums = tie(hidden_far.got, hidden_end.parts, sums)

        def passed(sums, carry=None):
            for total in sums:
                carry = plan.onward((total if carry is None else total + carry.astype(F32)).astype(BF16))
            return carry

        hidden_far.add().send()
        hidden_end.send()
        carry = passed(sums[1:])
        hidden_far.got, hidden_end.got = tie(hidden_far.got, hidden_end.got)

        hidden_end.add().send()
        down = plan.down(hidden_far.finish())
        hidden_end.got, carry, down = tie(hidden_end.got, carry, down)

        hidden, sums_far = tie(hidden_end.finish(), plan.both_cores(down, capacity))
        carry = passed(sums_far, carry)
        down = plan.down(hidden)
        mine, theirs = plan.by_core(down, capacity)
        theirs = plan.across(theirs.astype(BF16))
        carry, mine = tie(carry, mine)
        carry = passed(list(mine + theirs.astype(F32)), carry)

    total = sums[0] if carry is None else sums[0] + carry.astype(F32)
    total = total.astype(BF16)
    total = jnp.concatenate([total, plan.across(total)], 0)
    source = jnp.concatenate([row, row_other])
    pick = (lax.iota(jnp.int32, local_rows)[:, None] == source[None, :]).astype(BF16)
    return most, jnp.dot(pick, total, preferred_element_type=F32).astype(BF16)


def per_device(mesh, tokens, draft_counts, exit_layers, exit_gains, gate_weight, up_weight, down_weight):
    col_devices = mesh.shape["col"]
    chips = col_devices // 2
    local_rows = tokens.shape[0]
    sequences = local_rows // DRAFT
    capacity = local_rows * 3 // 4

    def run(most, skip, capacity, staged):
        me = lax.axis_index("col")
        others = lax.ppermute(tokens, "col", [(i, i ^ 1) for i in range(col_devices)])
        table = draft_counts * exit_gains.shape[0] + exit_layers
        table = jnp.concatenate([lax.dynamic_slice_in_dim(table, d * sequences, sequences) for d in (me, me ^ 1)])
        counts, exits = table // exit_gains.shape[0], table % exit_gains.shape[0]
        return block(
            skip, capacity, staged, mesh, most, counts, exits, tokens, others,
            exit_gains, gate_weight, up_weight, down_weight,
        )

    most = jnp.max(jnp.sum(draft_counts.reshape(chips, -1), axis=1))
    most, out = run(most, 0, capacity, chips >= 4)
    return lax.cond(
        most > 2 * capacity,
        lambda done: done + run(most, 2 * capacity, local_rows - capacity, False)[1],
        lambda done: done,
        out,
    )


def solution(mesh):
    return jax.shard_map(
        functools.partial(per_device, mesh),
        mesh=mesh,
        in_specs=(
            P("col", "row"),
            P(),
            P(),
            P(None, "row"),
            P("row", "col"),
            P("row", "col"),
            P("col", "row"),
        ),
        out_specs=P("col", "row"),
        check_vma=False,
    )
```
